32 devices in a mesh: batch: 2 (over y), region: 4 (over z), scen: 2 (over x), row: 2 (over core).
Axes of the slice: x: 2, y: 2, z: 4, core: 2. Of those that a mesh axis runs over, the one named last changes fastest.
Arguments:
- kkt_inverse: bfloat16 [4, 1536, 1536], P('region', 'row'), may hold values from -0.25 to 1.25, as said below
- bus_load: bfloat16 [4, 1536, 1024], P('region', None, ('batch', 'scen', 'row')), parts along dimension 2, may hold values from -6 to 6
- bus_limit: float32 [4, 1536], P('region'), may hold values from 0.3 to 3
- copy_local: int32 [4, 128], P('region'), may hold values from 0 to 1535, as said below
- copy_dest: int32 [4, 128], P('region'), may hold values from 0 to 3, as said below
- copy_slot: int32 [4, 128], P('region'), may hold values from 0 to 63, as said below
- copy_key: int32 [4, 128], P('region'), may hold values from 0 to 63
- own_key: int32 [4, 4, 64], P('region'), may hold values from -1 to 63, as said below
Outputs:
- dispatch: float32 [4, 1536, 1024], P('region', None, ('batch', 'scen', 'row')), parts along dimension 2
- scaled_duals: float32 [4, 128, 1024], P('region', None, ('batch', 'scen', 'row')), parts along dimension 2
The draws below stay inside these ranges and needn't reach their ends.
There are 2 independent parts, one for each index of `batch`. The reference program is written for one: setup_inputs(seed, part) draws one part's arguments, and reference() takes and returns one part's arrays. A program takes and returns all parts, laid end to end along the dimension named above; an argument that names none is the same for every part. Nothing has to cross between parts.
Inputs may be any that keep to these rules, and one draw needn't show every extreme that they name: `copy_local`: the 128 local buses of one region's copies are distinct. `copy_dest`: A region sends at most 64 copies to one owner; in every draw one owner receives exactly 64 copies from every region. `copy_slot`: within one region, copies with the same owner have distinct slots. own_key[o, r, s] equals copy_key[r, k] for the copy k of region r with copy_dest o and copy_slot s, and -1 where region r has no such copy. `kkt_inverse`: each matrix has a diagonal of 0.75 to 1.25 and independent off-diagonal entries.
All inputs are finite; a program needn't handle non-finite values.
Results may differ from the reference program's by a relative error of at most 0.0026.
Values may be sent and summed in bfloat16 or wider, within the bound.
A program may use at most 64 MiB of HBM per device.

```python
import math
import jax
import jax.numpy as jnp
from jax import lax

NB = 1536
KB = 128
GO = 64
ITERS = 3
REGIONS = 4
SCEN = 512
CAP = 64


def build_tables(key):
    key_local = jax.random.fold_in(key, 101)
    key_busy = jax.random.fold_in(key, 202)
    key_pool = jax.random.fold_in(key, 303)
    key_order = jax.random.fold_in(key, 404)
    key_pick = jax.random.fold_in(key, 505)
    key_shuffle = jax.random.fold_in(key, 808)
    region_ids = jnp.arange(REGIONS, dtype=jnp.int32)
    busy_owner = jax.random.randint(key_busy, (), 0, REGIONS).astype(jnp.int32)
    others = ((busy_owner + 1 + jnp.arange(REGIONS - 1, dtype=jnp.int32)) % REGIONS).astype(jnp.int32)
    pool_size = (REGIONS - 1) * CAP

    def one_region(region_index):
        inner = (1 + jax.random.permutation(jax.random.fold_in(key_local, region_index), NB - 2)[:KB - 2]).astype(jnp.int32)
        bus_all = jnp.concatenate([jnp.zeros((1,), jnp.int32), jnp.full((1,), NB - 1, jnp.int32), inner])
        bus_pick = bus_all[jax.random.permutation(jax.random.fold_in(key_shuffle, region_index), KB)]
        forced = (region_index % (REGIONS - 1) * CAP).astype(jnp.int32)
        rest = jax.random.permutation(jax.random.fold_in(key_pool, region_index), pool_size - 1)[:KB - CAP - 1].astype(jnp.int32)
        rest = ((forced + 1 + rest) % pool_size).astype(jnp.int32)
        chosen = jnp.concatenate([forced[None], rest])
        dest_row = jnp.concatenate([jnp.full((CAP,), busy_owner, jnp.int32), others[chosen // CAP]])
        slot_row = jnp.concatenate([jnp.arange(CAP, dtype=jnp.int32), (chosen % CAP).astype(jnp.int32)])
        reorder = jax.random.permutation(jax.random.fold_in(key_order, region_index), KB)
        return (bus_pick, dest_row[reorder], slot_row[reorder])
    bus_table, dest_table, slot_table = jax.vmap(one_region)(region_ids)
    key_table = jax.random.randint(key_pick, (REGIONS, KB), 0, GO).astype(jnp.int32)
    source_ids = jnp.broadcast_to(region_ids[:, None], (REGIONS, KB))
    owner_table = jnp.full((REGIONS, REGIONS, CAP), -1, jnp.int32).at[dest_table, source_ids, slot_table].set(key_table)
    return (bus_table, dest_table, slot_table, key_table, owner_table)


def draw_copy_local(key, part):
    return build_tables(key)[0]


def draw_copy_dest(key, part):
    return build_tables(key)[1]


def draw_copy_slot(key, part):
    return build_tables(key)[2]


def draw_copy_key(key, part):
    return build_tables(key)[3]


def draw_own_key(key, part):
    return build_tables(key)[4]


def draw_kkt_inverse(key, part):
    key_diag = jax.random.fold_in(key, 606)
    key_off = jax.random.fold_in(key, 707)
    diag_vals = jax.random.uniform(key_diag, (REGIONS, NB), jnp.float32, 0.75, 1.25)
    spread = 0.5 / NB ** 0.5
    off_vals = jax.random.normal(key_off, (REGIONS, NB, NB), jnp.float32) * spread
    off_vals = jnp.clip(off_vals, -0.25, 0.25)
    identity = jnp.eye(NB, dtype=jnp.float32)
    whole_matrix = off_vals * (1.0 - identity) + identity * diag_vals[:, :, None]
    return whole_matrix.astype(jnp.bfloat16)


def levels(key, dims, shards, low, largest):
    def one(dim, parts):
        heights = jax.random.uniform(jax.random.fold_in(jax.random.fold_in(key, 6), dim), (parts,), jnp.float32, low / len(shards), largest / len(shards))
        return jnp.repeat(jnp.exp(heights), dims[dim] // parts).reshape((-1,) + (1,) * (len(dims) - dim - 1))

    level = one(*shards[0])
    for cut in shards[1:]:
        level = level * one(*cut)
    return level


def centred(key, extent, scale, limit, split=(), held_as=jnp.bfloat16):
    factor_of = levels(key, extent, split, -0.22, 0.18) if split else 1.0
    array = jax.random.normal(key, extent, jnp.float32) * scale * factor_of
    return jnp.minimum(jnp.maximum(array, -limit), limit).astype(held_as)


def setup_inputs(seed: int = 0, part: int = 0) -> dict:
    arg_keys = jax.random.split(jax.random.key(seed), 9)
    part_keys = jax.random.split(jax.random.fold_in(arg_keys[8], part), 9)
    return {
        "kkt_inverse": draw_kkt_inverse(jax.random.fold_in(arg_keys[8], 71), part),
        "bus_load": centred(part_keys[1], (REGIONS, NB, SCEN), 1.0, 6.0, ((0, 4), (2, 4))),
        "bus_limit": jnp.clip(jnp.exp(math.log(3.0) - 2.3025851 * jax.random.uniform(arg_keys[2], (REGIONS, NB), jnp.float32) ** levels(arg_keys[2], (REGIONS, NB), ((0, 4),), -0.2, 0.2)), 0.3, 3.0),
        "copy_local": draw_copy_local(jax.random.fold_in(arg_keys[8], 71), part),
        "copy_dest": draw_copy_dest(jax.random.fold_in(arg_keys[8], 71), part),
        "copy_slot": draw_copy_slot(jax.random.fold_in(arg_keys[8], 71), part),
        "copy_key": draw_copy_key(jax.random.fold_in(arg_keys[8], 71), part),
        "own_key": draw_own_key(jax.random.fold_in(arg_keys[8], 71), part),
    }


PENALTY = 1.0
PROXIMAL = 0.5


def scatter_region(local_rows, values):
    return jnp.zeros((NB, SCEN), jnp.float32).at[local_rows].add(values)


def gather_region(region_field, local_rows):
    return region_field[local_rows]


def pack_region(row_ids, values):
    return jnp.zeros((REGIONS * CAP, SCEN), jnp.float32).at[row_ids].set(values)


def solve_region(matrix_pair):
    return jnp.dot(matrix_pair[0], matrix_pair[1], preferred_element_type=jnp.float32)


def reference(kkt_inverse, bus_load, bus_limit, copy_local, copy_dest, copy_slot, copy_key, own_key):
    send_rows = (copy_dest * CAP + copy_slot).astype(jnp.int32)
    fixed_keys = jnp.where(own_key >= 0, own_key, GO).astype(jnp.int32)
    owner_ids = jnp.arange(REGIONS, dtype=jnp.int32)[None, :, None]
    seg_ids = (owner_ids * (GO + 1) + jnp.transpose(fixed_keys, (1, 0, 2))).reshape(-1)
    lookup = (copy_dest * (GO + 1) + copy_key).reshape(-1).astype(jnp.int32)
    ones_col = jnp.ones((seg_ids.shape[0],), jnp.float32)
    counts = jax.ops.segment_sum(ones_col, seg_ids, num_segments=REGIONS * (GO + 1))
    dispatch = jnp.zeros((REGIONS, NB, SCEN), jnp.float32)
    dual_vals = jnp.zeros((REGIONS, KB, SCEN), jnp.float32)
    consensus = jnp.zeros((REGIONS, KB, SCEN), jnp.float32)
    for iteration in range(ITERS):
        boundary = jax.vmap(scatter_region)(copy_local, consensus - dual_vals)
        drive_cols = (bus_load.astype(jnp.float32) + PROXIMAL * dispatch + PENALTY * boundary).astype(jnp.bfloat16)
        solved = lax.map(solve_region, (kkt_inverse, drive_cols))
        dispatch = jnp.clip(solved, -bus_limit[:, :, None], bus_limit[:, :, None])
        at_copies = jax.vmap(gather_region)(dispatch, copy_local)
        shared = at_copies + dual_vals
        packed = jax.vmap(pack_region)(send_rows, shared)
        totals = jax.ops.segment_sum(packed.reshape(-1, SCEN), seg_ids, num_segments=REGIONS * (GO + 1))
        averages = totals / jnp.maximum(counts, 1.0)[:, None]
        consensus = averages[lookup].reshape(REGIONS, KB, SCEN)
        dual_vals = dual_vals + at_copies - consensus
    return dispatch, dual_vals
```

```python
import functools

import jax
import jax.numpy as jnp
from jax import lax
from jax.experimental import pallas as pl
from jax.experimental.pallas import tpu as pltpu
from jax.sharding import PartitionSpec as P

ITERS = 3
PENALTY = 1.0
PROXIMAL = 0.5

MESH = pl.DeviceIdType.MESH
F32 = jnp.float32
BF16 = jnp.bfloat16


def wide(a, b):
    return jnp.dot(a, b, preferred_element_type=F32)


def halves(x):
    hi = x.astype(BF16)
    lo = (x - hi.astype(F32)).astype(BF16)
    return hi, lo


def kernel(
    regions, rows, step, link,
    inv_ref, load_ref, limit_ref, local_ref, dest_ref, key_ref,
    disp_ref, dual_ref,
    full, first_rhs, part, limits, load_in, prox_in, columns, drive, pick, gathered,
    outbox, inbox, id_out, id_in,
    own_sem, full_send, full_recv, id_send, id_recv, box_send, box_recv,
):
    me = lax.axis_index("region")
    row = lax.axis_index("row")
    half = inv_ref.shape[1]
    buses, cols = load_ref.shape[1], load_ref.shape[2]
    copies = local_ref.shape[1]
    chunks = half // step
    first_row = row * half
    peers = [lax.rem(me + j, regions) for j in range(1, regions)]
    mates = [lax.rem(row + j, rows) for j in range(1, rows)]

    barrier = pltpu.get_barrier_semaphore()
    for mate in mates:
        pl.semaphore_signal(barrier, inc=1, device_id={"row": mate}, device_id_type=MESH)
    for peer in peers:
        pl.semaphore_signal(barrier, inc=1, device_id={"region": peer}, device_id_type=MESH)

    own_copies = []
    for c in range(chunks):
        copy = pltpu.make_async_copy(
            inv_ref.at[0, pl.ds(c * step, step)],
            full.at[pl.ds(pl.multiple_of(first_row + c * step, step), step)],
            own_sem.at[c],
        )
        copy.start()
        own_copies.append(copy)
    ids = (key_ref[...] * regions + dest_ref[...]).astype(F32)
    id_out[...] = jnp.broadcast_to(ids, id_out.shape)

    pl.semaphore_wait(barrier, len(mates) + len(peers))
    full_copies = []
    for c in range(chunks):
        for j, mate in enumerate(mates):
            copy = pltpu.make_async_remote_copy(
                src_ref=inv_ref.at[0, pl.ds(c * step, step)],
                dst_ref=full.at[pl.ds(pl.multiple_of(first_row + c * step, step), step)],
                send_sem=full_send.at[j, c],
                recv_sem=full_recv.at[j, c],
                device_id={"row": mate},
                device_id_type=MESH,
            )
            copy.start()
            full_copies.append((c, j, copy))
    id_copies = []
    for j, peer in enumerate(peers):
        copy = pltpu.make_async_remote_copy(
            src_ref=id_out,
            dst_ref=id_in.at[j],
            send_sem=id_send.at[j],
            recv_sem=id_recv.at[j],
            device_id={"region": peer},
            device_id_type=MESH,
        )
        copy.start()
        id_copies.append(copy)

    local_row = local_ref[...].astype(F32)
    local_col = jnp.transpose(jnp.broadcast_to(local_row, (copies, copies)))[:, :1]
    bus_lane = lax.broadcasted_iota(jnp.int32, (copies, buses), 1).astype(F32)
    pick[...] = jnp.where(bus_lane == local_col, 1.0, 0.0).astype(BF16)
    bus_sub = lax.broadcasted_iota(jnp.int32, (buses, copies), 0).astype(F32)
    place = jnp.where(bus_sub == local_row, 1.0, 0.0).astype(BF16)
    first_rhs[:, :cols] = load_ref[0]
    first_rhs[:, cols:] = place
    inner = 1.0 - wide(place, jnp.ones((copies, cols), BF16))
    load_in[...] = (load_ref[0].astype(F32) * inner).astype(BF16)
    prox_in[...] = PROXIMAL * inner
    for block in range(0, buses, cols):
        piece = jnp.broadcast_to(limit_ref[:, block:block + cols], (cols, cols))
        limits[block:block + cols, :] = jnp.transpose(piece)
    load_at = wide(pick[...], load_ref[0])
    top = limits[...].astype(BF16)
    rest = limits[...] - top.astype(F32)
    mid = rest.astype(BF16)
    low = (rest - mid.astype(F32)).astype(BF16)
    limit_at = wide(pick[...], top) + wide(pick[...], mid) + wide(pick[...], low)

    gathered[...] = jnp.zeros_like(gathered)

    def first_chunk(at):
        at = pl.multiple_of(at, step)
        rows_at = pl.ds(at, step)
        prod = wide(full[rows_at, :], first_rhs[...])
        picked = prod[:, cols:].astype(BF16)
        columns[rows_at, :] = picked
        bound = limits[rows_at, :]
        value = jnp.clip(prod[:, :cols], -bound, bound)
        disp_ref[0, rows_at, :] = value
        hi, lo = halves(value)
        gathered[...] += wide(pick[:, rows_at], jnp.concatenate([hi, lo, picked], axis=1))

    for c in range(chunks):
        own_copies[c].wait()
        first_chunk(first_row + c * step)
    for c, j, copy in full_copies:
        copy.wait()
        first_chunk(lax.rem(row + rows - j - 1, rows) * half + c * step)
    at_copies = gathered[:, :cols] + gathered[:, cols:2 * cols]
    columns_at = gathered[:, 2 * cols:].astype(BF16)
    duals = jnp.zeros((copies, cols), F32)

    matches = None
    for it in range(ITERS):
        shared = at_copies + duals
        outbox[it] = shared.astype(link)
        box_copies = []
        for j, peer in enumerate(peers):
            copy = pltpu.make_async_remote_copy(
                src_ref=outbox.at[it],
                dst_ref=inbox.at[it, j],
                send_sem=box_send.at[it, j],
                recv_sem=box_recv.at[it, j],
                device_id={"region": peer},
                device_id_type=MESH,
            )
            copy.start()
            box_copies.append(copy)
        if it > 0:
            value = part[...] + wide(columns[...], drive_at)
            disp_ref[0] = jnp.clip(value, -limits[...], limits[...])
        if it < ITERS - 1:
            drive[...] = (load_in[...].astype(F32) + prox_in[...] * disp_ref[0]).astype(BF16)
            gathered[:, :2 * cols] = jnp.zeros((copies, 2 * cols), F32)

            def bulk(i, carry):
                rows_at = pl.ds(pl.multiple_of(i * step, step), step)
                prod = wide(full[rows_at, :], drive[...])
                part[rows_at, :] = prod
                hi, lo = halves(prod)
                gathered[:, :2 * cols] += wide(pick[:, rows_at], jnp.concatenate([hi, lo], axis=1))
                return carry

            lax.fori_loop(0, buses // step, bulk, 0)
        if matches is None:
            id_col = jnp.transpose(jnp.broadcast_to(ids, (copies, copies)))[:, :1]
            for copy in id_copies:
                copy.wait()
            matches = [jnp.where(id_col == ids, 1.0, 0.0).astype(BF16)]
            for j in range(regions - 1):
                matches.append(jnp.where(id_col == id_in[j, :1, :], 1.0, 0.0).astype(BF16))
            tally = functools.reduce(
                lambda a, b: a + b, [wide(m, jnp.ones((copies, cols), BF16)) for m in matches]
            )
            tally = jnp.maximum(tally, 1.0)
        hi, lo = halves(shared)
        total = wide(matches[0], hi) + wide(matches[0], lo)
        for j, copy in enumerate(box_copies):
            copy.wait()
            if link == F32:
                hi, lo = halves(inbox[it, j])
                total += wide(matches[j + 1], hi) + wide(matches[j + 1], lo)
            else:
                total += wide(matches[j + 1], inbox[it, j])
        consensus = total / tally
        duals = duals + at_copies - consensus
        if it < ITERS - 1:
            boundary = consensus - duals
            drive_at = (load_at + PROXIMAL * at_copies + PENALTY * boundary).astype(BF16)
            solved_at = gathered[:, :cols] + gathered[:, cols:2 * cols] + wide(columns_at, drive_at)
            at_copies = jnp.clip(solved_at, -limit_at, limit_at)
    dual_ref[0] = duals


def chunk_rows(half):
    for step in (256, 128):
        if half % step == 0:
            return step
    return half


LINK = F32


def per_device(
    kkt_inverse, bus_load, bus_limit, copy_local, copy_dest, copy_slot, copy_key, own_key
):
    regions = lax.axis_size("region")
    rows = lax.axis_size("row")
    half = kkt_inverse.shape[1]
    buses, cols = bus_load.shape[1], bus_load.shape[2]
    copies = copy_local.shape[1]
    step = chunk_rows(half)
    chunks = half // step
    dma = pltpu.SemaphoreType.DMA
    vmem = pl.BlockSpec(memory_space=pltpu.VMEM)
    return pl.pallas_call(
        functools.partial(kernel, regions, rows, step, LINK),
        out_shape=(
            jax.ShapeDtypeStruct((1, buses, cols), F32),
            jax.ShapeDtypeStruct((1, copies, cols), F32),
        ),
        in_specs=[pl.BlockSpec(memory_space=pl.ANY)] + [vmem] * 5,
        out_specs=(vmem, vmem),
        scratch_shapes=[
            pltpu.VMEM((buses, buses), BF16),
            pltpu.VMEM((buses, cols + copies), BF16),
            pltpu.VMEM((buses, cols), F32),
            pltpu.VMEM((buses, cols), F32),
            pltpu.VMEM((buses, cols), BF16),
            pltpu.VMEM((buses, cols), F32),
            pltpu.VMEM((buses, copies), BF16),
            pltpu.VMEM((buses, cols), BF16),
            pltpu.VMEM((copies, buses), BF16),
            pltpu.VMEM((copies, 2 * cols + copies), F32),
            pltpu.VMEM((ITERS, copies, cols), LINK),
            pltpu.VMEM((ITERS, regions - 1, copies, cols), LINK),
            pltpu.VMEM((8, copies), F32),
            pltpu.VMEM((regions - 1, 8, copies), F32),
            dma((chunks,)),
            dma((rows - 1, chunks)),
            dma((rows - 1, chunks)),
            dma((regions - 1,)),
            dma((regions - 1,)),
            dma((ITERS, regions - 1)),
            dma((ITERS, regions - 1)),
        ],
        compiler_params=pltpu.CompilerParams(
            collective_id=0, has_side_effects=True, vmem_limit_bytes=48 * 1024 * 1024
        ),
    )(kkt_inverse, bus_load, bus_limit, copy_local, copy_dest, copy_key)


def solution(mesh):
    return jax.shard_map(
        per_device,
        mesh=mesh,
        in_specs=(
            P("region", "row", None),
            P("region", None, ("batch", "scen", "row")),
            P("region", None),
            P("region", None),
            P("region", None),
            P("region", None),
            P("region", None),
            P("region", None, None),
        ),
        out_specs=(
            P("region", None, ("batch", "scen", "row")),
            P("region", None, ("batch", "scen", "row")),
        ),
        check_vma=False,
    )
```

```python
import functools

import jax
import jax.numpy as jnp
from jax import lax
from jax.experimental import pallas as pl
from jax.experimental.pallas import tpu as pltpu
from jax.sharding import PartitionSpec as P

ITERS = 3
PENALTY = 1.0
PROXIMAL = 0.5

MESH = pl.DeviceIdType.MESH
F32 = jnp.float32
BF16 = jnp.bfloat16


def wide(a, b):
    return jnp.dot(a, b, preferred_element_type=F32)


def halves(x):
    hi = x.astype(BF16)
    lo = (x - hi.astype(F32)).astype(BF16)
    return hi, lo


def kernel(
    regions, rows, step, link,
    inv_ref, load_hbm, limit_hbm, local_hbm, dest_hbm, key_hbm,
    disp_ref, dual_ref,
    load_ref, limit_ref, local_ref, dest_ref, key_ref,
    full, first_rhs, part, limits, load_in, prox_in, columns, drive, pick, gathered,
    outbox, inbox, id_out, id_in,
    in_sem, own_sem, full_send, full_recv, id_send, id_recv, box_send, box_recv,
):
    me = lax.axis_index("region")
    row = lax.axis_index("row")
    half = inv_ref.shape[1]
    buses, cols = load_ref.shape[1], load_ref.shape[2]
    copies = local_ref.shape[1]
    chunks = half // step
    first_row = row * half
    peers = [lax.rem(me + j, regions) for j in range(1, regions)]
    mates = [lax.rem(row + j, rows) for j in range(1, rows)]

    barrier = pltpu.get_barrier_semaphore()
    for mate in mates:
        pl.semaphore_signal(barrier, inc=1, device_id={"row": mate}, device_id_type=MESH)
    for peer in peers:
        pl.semaphore_signal(barrier, inc=1, device_id={"region": peer}, device_id_type=MESH)

    in_copies = []
    for n, (source, target) in enumerate((
        (key_hbm, key_ref), (dest_hbm, dest_ref), (local_hbm, local_ref),
        (limit_hbm, limit_ref), (load_hbm, load_ref),
    )):
        copy = pltpu.make_async_copy(source, target, in_sem.at[n])
        copy.start()
        in_copies.append(copy)
    own_copies = []
    for c in range(chunks):
        copy = pltpu.make_async_copy(
            inv_ref.at[0, pl.ds(c * step, step)],
            full.at[pl.ds(pl.multiple_of(first_row + c * step, step), step)],
            own_sem.at[c],
        )
        copy.start()
        own_copies.append(copy)
    pl.semaphore_wait(barrier, len(mates) + len(peers))
    full_copies = []
    for c in range(chunks):
        for j, mate in enumerate(mates):
            copy = pltpu.make_async_remote_copy(
                src_ref=inv_ref.at[0, pl.ds(c * step, step)],
                dst_ref=full.at[pl.ds(pl.multiple_of(first_row + c * step, step), step)],
                send_sem=full_send.at[j, c],
                recv_sem=full_recv.at[j, c],
                device_id={"row": mate},
                device_id_type=MESH,
            )
            copy.start()
            full_copies.append((c, j, copy))
    for copy in in_copies:
        copy.wait()
    ids = (key_ref[...] * regions + dest_ref[...]).astype(F32)
    id_out[...] = jnp.broadcast_to(ids, id_out.shape)
    id_copies = []
    for j, peer in enumerate(peers):
        copy = pltpu.make_async_remote_copy(
            src_ref=id_out,
            dst_ref=id_in.at[j],
            send_sem=id_send.at[j],
            recv_sem=id_recv.at[j],
            device_id={"region": peer},
            device_id_type=MESH,
        )
        copy.start()
        id_copies.append(copy)

    local_row = local_ref[...].astype(F32)
    local_col = jnp.transpose(jnp.broadcast_to(local_row, (copies, copies)))[:, :1]
    bus_lane = lax.broadcasted_iota(jnp.int32, (copies, buses), 1).astype(F32)
    pick[...] = jnp.where(bus_lane == local_col, 1.0, 0.0).astype(BF16)
    bus_sub = lax.broadcasted_iota(jnp.int32, (buses, copies), 0).astype(F32)
    place = jnp.where(bus_sub == local_row, 1.0, 0.0).astype(BF16)
    first_rhs[:, :cols] = load_ref[0]
    first_rhs[:, cols:] = place
    inner = 1.0 - wide(place, jnp.ones((copies, cols), BF16))
    load_in[...] = (load_ref[0].astype(F32) * inner).astype(BF16)
    prox_in[...] = PROXIMAL * inner
    for block in range(0, buses, cols):
        piece = jnp.broadcast_to(limit_ref[:, block:block + cols], (cols, cols))
        limits[block:block + cols, :] = jnp.transpose(piece)
    load_at = wide(pick[...], load_ref[0])
    top = limits[...].astype(BF16)
    rest = limits[...] - top.astype(F32)
    mid = rest.astype(BF16)
    low = (rest - mid.astype(F32)).astype(BF16)
    limit_at = wide(pick[...], top) + wide(pick[...], mid) + wide(pick[...], low)

    gathered[...] = jnp.zeros_like(gathered)

    def first_chunk(at):
        at = pl.multiple_of(at, step)
        rows_at = pl.ds(at, step)
        prod = wide(full[rows_at, :], first_rhs[...])
        picked = prod[:, cols:].astype(BF16)
        columns[rows_at, :] = picked
        bound = limits[rows_at, :]
        value = jnp.clip(prod[:, :cols], -bound, bound)
        disp_ref[0, rows_at, :] = value
        hi, lo = halves(value)
        gathered[...] += wide(pick[:, rows_at], jnp.concatenate([hi, lo, picked], axis=1))

    for c in range(chunks):
        own_copies[c].wait()
        first_chunk(first_row + c * step)
    for c, j, copy in full_copies:
        copy.wait()
        first_chunk(lax.rem(row + rows - j - 1, rows) * half + c * step)
    at_copies = gathered[:, :cols] + gathered[:, cols:2 * cols]
    columns_at = gathered[:, 2 * cols:].astype(BF16)
    duals = jnp.zeros((copies, cols), F32)

    matches = None
    for it in range(ITERS):
        shared = at_copies + duals
        outbox[it] = shared.astype(link)
        box_copies = []
        for j, peer in enumerate(peers):
            copy = pltpu.make_async_remote_copy(
                src_ref=outbox.at[it],
                dst_ref=inbox.at[it, j],
                send_sem=box_send.at[it, j],
                recv_sem=box_recv.at[it, j],
                device_id={"region": peer},
                device_id_type=MESH,
            )
            copy.start()
            box_copies.append(copy)
        if it > 0:
            value = part[...] + wide(columns[...], drive_at)
            disp_ref[0] = jnp.clip(value, -limits[...], limits[...])
        if it < ITERS - 1:
            drive[...] = (load_in[...].astype(F32) + prox_in[...] * disp_ref[0]).astype(BF16)
            for at in range(0, buses, half):
                part[at:at + half, :] = wide(full[at:at + half, :], drive[...])
            hi, lo = halves(part[...])
            gathered[:, :2 * cols] = wide(pick[...], jnp.concatenate([hi, lo], axis=1))
        if matches is None:
            id_col = jnp.transpose(jnp.broadcast_to(ids, (copies, copies)))[:, :1]
            for copy in id_copies:
                copy.wait()
            matches = [jnp.where(id_col == ids, 1.0, 0.0).astype(BF16)]
            for j in range(regions - 1):
                matches.append(jnp.where(id_col == id_in[j, :1, :], 1.0, 0.0).astype(BF16))
            tally = functools.reduce(
                lambda a, b: a + b, [wide(m, jnp.ones((copies, cols), BF16)) for m in matches]
            )
            tally = jnp.maximum(tally, 1.0)
        hi, lo = halves(shared)
        total = wide(matches[0], hi) + wide(matches[0], lo)
        for j, copy in enumerate(box_copies):
            copy.wait()
            if link == F32:
                hi, lo = halves(inbox[it, j])
                total += wide(matches[j + 1], hi) + wide(matches[j + 1], lo)
            else:
                total += wide(matches[j + 1], inbox[it, j])
        consensus = total / tally
        duals = duals + at_copies - consensus
        if it < ITERS - 1:
            boundary = consensus - duals
            drive_at = (load_at + PROXIMAL * at_copies + PENALTY * boundary).astype(BF16)
            solved_at = gathered[:, :cols] + gathered[:, cols:2 * cols] + wide(columns_at, drive_at)
            at_copies = jnp.clip(solved_at, -limit_at, limit_at)
    dual_ref[0] = duals


def chunk_rows(half):
    for step in (256, 128):
        if half % step == 0:
            return step
    return half


LINK = BF16


def per_device(
    kkt_inverse, bus_load, bus_limit, copy_local, copy_dest, copy_slot, copy_key, own_key
):
    regions = lax.axis_size("region")
    rows = lax.axis_size("row")
    half = kkt_inverse.shape[1]
    buses, cols = bus_load.shape[1], bus_load.shape[2]
    copies = copy_local.shape[1]
    step = chunk_rows(half)
    chunks = half // step
    dma = pltpu.SemaphoreType.DMA
    vmem = pl.BlockSpec(memory_space=pltpu.VMEM)
    return pl.pallas_call(
        functools.partial(kernel, regions, rows, step, LINK),
        out_shape=(
            jax.ShapeDtypeStruct((1, buses, cols), F32),
            jax.ShapeDtypeStruct((1, copies, cols), F32),
        ),
        in_specs=[pl.BlockSpec(memory_space=pltpu.HBM)] * 6,
        out_specs=(vmem, vmem),
        scratch_shapes=[
            pltpu.VMEM(bus_load.shape, bus_load.dtype),
            pltpu.VMEM(bus_limit.shape, bus_limit.dtype),
            pltpu.VMEM(copy_local.shape, copy_local.dtype),
            pltpu.VMEM(copy_dest.shape, copy_dest.dtype),
            pltpu.VMEM(copy_key.shape, copy_key.dtype),
            pltpu.VMEM((buses, buses), BF16),
            pltpu.VMEM((buses, cols + copies), BF16),
            pltpu.VMEM((buses, cols), F32),
            pltpu.VMEM((buses, cols), F32),
            pltpu.VMEM((buses, cols), BF16),
            pltpu.VMEM((buses, cols), F32),
            pltpu.VMEM((buses, copies), BF16),
            pltpu.VMEM((buses, cols), BF16),
            pltpu.VMEM((copies, buses), BF16),
            pltpu.VMEM((copies, 2 * cols + copies), F32),
            pltpu.VMEM((ITERS, copies, cols), LINK),
            pltpu.VMEM((ITERS, regions - 1, copies, cols), LINK),
            pltpu.VMEM((8, copies), F32),
            pltpu.VMEM((regions - 1, 8, copies), F32),
            dma((5,)),
            dma((chunks,)),
            dma((rows - 1, chunks)),
            dma((rows - 1, chunks)),
            dma((regions - 1,)),
            dma((regions - 1,)),
            dma((ITERS, regions - 1)),
            dma((ITERS, regions - 1)),
        ],
        compiler_params=pltpu.CompilerParams(
            collective_id=0, has_side_effects=True, vmem_limit_bytes=48 * 1024 * 1024
        ),
    )(*[pltpu.with_memory_space_constraint(x, pltpu.HBM) for x in (kkt_inverse, bus_load, bus_limit, copy_local, copy_dest, copy_key)])


def solution(mesh):
    return jax.shard_map(
        per_device,
        mesh=mesh,
        in_specs=(
            P("region", "row", None),
            P("region", None, ("batch", "scen", "row")),
            P("region", None),
            P("region", None),
            P("region", None),
            P("region", None),
            P("region", None),
            P("region", None, None),
        ),
        out_specs=(
            P("region", None, ("batch", "scen", "row")),
            P("region", None, ("batch", "scen", "row")),
        ),
        check_vma=False,
    )
```

```python
import functools

import jax
import jax.numpy as jnp
from jax import lax
from jax.experimental import pallas as pl
from jax.experimental.pallas import tpu as pltpu
from jax.sharding import PartitionSpec as P

ITERS = 3
PENALTY = 1.0
PROXIMAL = 0.5

MESH = pl.DeviceIdType.MESH
F32 = jnp.float32
BF16 = jnp.bfloat16
LINK = BF16


def wide(a, b):
    return jnp.dot(a, b, preferred_element_type=F32)


def halves(x):
    hi = x.astype(BF16)
    lo = (x - hi.astype(F32)).astype(BF16)
    return hi, lo


def kernel(
    regions, rows, step,
    inv_ref, load_hbm, limit_hbm, local_hbm, dest_hbm, key_hbm,
    disp_ref, dual_ref,
    load_ref, limit_ref, local_ref, dest_ref, key_ref,
    full, first_rhs, limits, load_in, prox_in, columns, drive, pick,
    rows_out, rows_in, rows_at_copies,
    outbox, inbox, id_out, id_in,
    in_sem, own_sem, full_send, full_recv, id_send, id_recv, box_send, box_recv, row_send, row_recv,
):
    me = lax.axis_index("region")
    row = lax.axis_index("row")
    half = inv_ref.shape[1]
    buses, cols = load_ref.shape[1], load_ref.shape[2]
    copies = local_ref.shape[1]
    chunks = half // step
    first_row = row * half
    peers = [lax.rem(me + j, regions) for j in range(1, regions)]
    mates = [lax.rem(row + j, rows) for j in range(1, rows)]

    barrier = pltpu.get_barrier_semaphore()
    for mate in mates:
        pl.semaphore_signal(barrier, inc=1, device_id={"row": mate}, device_id_type=MESH)
    for peer in peers:
        pl.semaphore_signal(barrier, inc=1, device_id={"region": peer}, device_id_type=MESH)

    in_copies = []
    for n, (source, target) in enumerate((
        (key_hbm, key_ref), (dest_hbm, dest_ref), (local_hbm, local_ref),
        (limit_hbm, limit_ref), (load_hbm, load_ref),
    )):
        copy = pltpu.make_async_copy(source, target, in_sem.at[n])
        copy.start()
        in_copies.append(copy)
    own_copies = []
    for c in range(chunks):
        copy = pltpu.make_async_copy(
            inv_ref.at[0, pl.ds(c * step, step)],
            full.at[pl.ds(pl.multiple_of(first_row + c * step, step), step)],
            own_sem.at[c],
        )
        copy.start()
        own_copies.append(copy)
    for copy in in_copies:
        copy.wait()
    ids = (key_ref[...] * regions + dest_ref[...]).astype(F32)
    id_out[...] = jnp.broadcast_to(ids, id_out.shape)
    local_row = local_ref[...].astype(F32)
    local_col = jnp.transpose(jnp.broadcast_to(local_row, (copies, copies)))[:, :1]
    bus_lane = lax.broadcasted_iota(jnp.int32, (copies, buses), 1).astype(F32)
    pick[...] = jnp.where(bus_lane == local_col, 1.0, 0.0).astype(BF16)
    bus_sub = lax.broadcasted_iota(jnp.int32, (buses, copies), 0).astype(F32)
    place = jnp.where(bus_sub == local_row, 1.0, 0.0).astype(BF16)
    first_rhs[:, :cols] = load_ref[0]
    first_rhs[:, cols:] = place
    inner = 1.0 - wide(place, jnp.ones((copies, cols), BF16))
    load_in[...] = (load_ref[0].astype(F32) * inner).astype(BF16)
    prox_in[...] = PROXIMAL * inner
    for block in range(0, buses, cols):
        piece = jnp.broadcast_to(limit_ref[:, block:block + cols], (cols, cols))
        limits[block:block + cols, :] = jnp.transpose(piece)
    load_at = wide(pick[...], load_ref[0])
    top = limits[...].astype(BF16)
    rest = limits[...] - top.astype(F32)
    mid = rest.astype(BF16)
    low = (rest - mid.astype(F32)).astype(BF16)
    limit_at = wide(pick[...], top) + wide(pick[...], mid) + wide(pick[...], low)

    for copy in own_copies:
        copy.wait()
    own_pick = pick[:, pl.ds(pl.multiple_of(first_row, cols), half)]
    rows_out[...] = wide(
        own_pick, full[pl.ds(pl.multiple_of(first_row, step), half), :]
    ).astype(BF16)
    pl.semaphore_wait(barrier, len(mates) + len(peers))
    row_copies = []
    for j, mate in enumerate(mates):
        copy = pltpu.make_async_remote_copy(
            src_ref=rows_out,
            dst_ref=rows_in.at[j],
            send_sem=row_send.at[j],
            recv_sem=row_recv.at[j],
            device_id={"row": mate},
            device_id_type=MESH,
        )
        copy.start()
        row_copies.append(copy)
    id_copies = []
    for j, peer in enumerate(peers):
        copy = pltpu.make_async_remote_copy(
            src_ref=id_out,
            dst_ref=id_in.at[j],
            send_sem=id_send.at[j],
            recv_sem=id_recv.at[j],
            device_id={"region": peer},
            device_id_type=MESH,
        )
        copy.start()
        id_copies.append(copy)

    full_copies = []
    for c in range(chunks):
        for j, mate in enumerate(mates):
            copy = pltpu.make_async_remote_copy(
                src_ref=inv_ref.at[0, pl.ds(c * step, step)],
                dst_ref=full.at[pl.ds(pl.multiple_of(first_row + c * step, step), step)],
                send_sem=full_send.at[j, c],
                recv_sem=full_recv.at[j, c],
                device_id={"row": mate},
                device_id_type=MESH,
            )
            copy.start()
            full_copies.append((c, j, copy))
    at_rows = rows_out[...]
    for j, copy in enumerate(row_copies):
        copy.wait()
        at_rows = at_rows + rows_in[j]
    rows_at_copies[...] = at_rows
    at_copies = jnp.clip(wide(rows_at_copies[...], load_ref[0]), -limit_at, limit_at)

    def first_chunk(at):
        at = pl.multiple_of(at, step)
        rows_at = pl.ds(at, step)
        prod = wide(full[rows_at, :], first_rhs[...])
        picked = prod[:, cols:].astype(BF16)
        columns[rows_at, :] = picked
        bound = limits[rows_at, :]
        value = jnp.clip(prod[:, :cols], -bound, bound)
        disp_ref[0, rows_at, :] = value

    duals = jnp.zeros((copies, cols), F32)

    matches = None
    for it in range(ITERS):
        shared = at_copies + duals
        outbox[it] = shared.astype(LINK)
        box_copies = []
        for j, peer in enumerate(peers):
            copy = pltpu.make_async_remote_copy(
                src_ref=outbox.at[it],
                dst_ref=inbox.at[it, j],
                send_sem=box_send.at[it, j],
                recv_sem=box_recv.at[it, j],
                device_id={"region": peer},
                device_id_type=MESH,
            )
            copy.start()
            box_copies.append(copy)
        if it == 0:
            for c in range(chunks):
                first_chunk(first_row + c * step)
            for c, j, copy in full_copies:
                copy.wait()
                first_chunk(lax.rem(row + rows - j - 1, rows) * half + c * step)
            columns_at = wide(rows_at_copies[...], first_rhs[:, cols:]).astype(BF16)
        else:
            for at in range(0, buses, half):
                value = wide(full[at:at + half, :], drive[...])
                value = value + wide(columns[at:at + half, :], drive_at)
                bound = limits[at:at + half, :]
                disp_ref[0, at:at + half, :] = jnp.clip(value, -bound, bound)
        if it < ITERS - 1:
            drive[...] = (load_in[...].astype(F32) + prox_in[...] * disp_ref[0]).astype(BF16)
            inner_at = wide(rows_at_copies[...], drive[...])
        if matches is None:
            id_col = jnp.transpose(jnp.broadcast_to(ids, (copies, copies)))[:, :1]
            for copy in id_copies:
                copy.wait()
            own_match = jnp.where(id_col == ids, 1.0, 0.0).astype(BF16)
            matches = jnp.concatenate([
                jnp.where(id_col == id_in[j, :1, :], 1.0, 0.0).astype(BF16)
                for j in range(regions - 1)
            ], axis=1)
            tally = wide(own_match, jnp.ones((copies, cols), BF16))
            tally += wide(matches, jnp.ones((matches.shape[1], cols), BF16))
            tally = jnp.maximum(tally, 1.0)
        hi, lo = halves(shared)
        total = wide(own_match, hi) + wide(own_match, lo)
        for copy in box_copies:
            copy.wait()
        total += wide(matches, inbox[it].reshape(matches.shape[1], cols))
        consensus = total / tally
        duals = duals + at_copies - consensus
        if it < ITERS - 1:
            boundary = consensus - duals
            drive_at = (load_at + PROXIMAL * at_copies + PENALTY * boundary).astype(BF16)
            solved_at = inner_at + wide(columns_at, drive_at)
            at_copies = jnp.clip(solved_at, -limit_at, limit_at)
    dual_ref[0] = duals


def chunk_rows(half):
    for step in (256, 128):
        if half % step == 0:
            return step
    return half


def per_device(
    kkt_inverse, bus_load, bus_limit, copy_local, copy_dest, copy_slot, copy_key, own_key
):
    regions = lax.axis_size("region")
    rows = lax.axis_size("row")
    half = kkt_inverse.shape[1]
    buses, cols = bus_load.shape[1], bus_load.shape[2]
    copies = copy_local.shape[1]
    step = chunk_rows(half)
    chunks = half // step
    dma = pltpu.SemaphoreType.DMA
    vmem = pl.BlockSpec(memory_space=pltpu.VMEM)
    return pl.pallas_call(
        functools.partial(kernel, regions, rows, step),
        out_shape=(
            jax.ShapeDtypeStruct((1, buses, cols), F32),
            jax.ShapeDtypeStruct((1, copies, cols), F32),
        ),
        in_specs=[pl.BlockSpec(memory_space=pltpu.HBM)] * 6,
        out_specs=(vmem, vmem),
        scratch_shapes=[
            pltpu.VMEM(bus_load.shape, bus_load.dtype),
            pltpu.VMEM(bus_limit.shape, bus_limit.dtype),
            pltpu.VMEM(copy_local.shape, copy_local.dtype),
            pltpu.VMEM(copy_dest.shape, copy_dest.dtype),
            pltpu.VMEM(copy_key.shape, copy_key.dtype),
            pltpu.VMEM((buses, buses), BF16),
            pltpu.VMEM((buses, cols + copies), BF16),
            pltpu.VMEM((buses, cols), F32),
            pltpu.VMEM((buses, cols), BF16),
            pltpu.VMEM((buses, cols), F32),
            pltpu.VMEM((buses, copies), BF16),
            pltpu.VMEM((buses, cols), BF16),
            pltpu.VMEM((copies, buses), BF16),
            pltpu.VMEM((copies, buses), BF16),
            pltpu.VMEM((rows - 1, copies, buses), BF16),
            pltpu.VMEM((copies, buses), BF16),
            pltpu.VMEM((ITERS, copies, cols), LINK),
            pltpu.VMEM((ITERS, regions - 1, copies, cols), LINK),
            pltpu.VMEM((8, copies), F32),
            pltpu.VMEM((regions - 1, 8, copies), F32),
            dma((5,)),
            dma((chunks,)),
            dma((rows - 1, chunks)),
            dma((rows - 1, chunks)),
            dma((regions - 1,)),
            dma((regions - 1,)),
            dma((ITERS, regions - 1)),
            dma((ITERS, regions - 1)),
            dma((rows - 1,)),
            dma((rows - 1,)),
        ],
        compiler_params=pltpu.CompilerParams(
            collective_id=0, has_side_effects=True, vmem_limit_bytes=48 * 1024 * 1024
        ),
    )(*[pltpu.with_memory_space_constraint(x, pltpu.HBM) for x in (kkt_inverse, bus_load, bus_limit, copy_local, copy_dest, copy_key)])


def solution(mesh):
    return jax.shard_map(
        per_device,
        mesh=mesh,
        in_specs=(
            P("region", "row", None),
            P("region", None, ("batch", "scen", "row")),
            P("region", None),
            P("region", None),
            P("region", None),
            P("region", None),
            P("region", None),
            P("region", None, None),
        ),
        out_specs=(
            P("region", None, ("batch", "scen", "row")),
            P("region", None, ("batch", "scen", "row")),
        ),
        check_vma=False,
    )
```
